256 devices in a mesh: seq: 32 (over z, y), tensor: 8 (over x, core).
Axes of the slice: x: 4, y: 4, z: 8, core: 2. Of those that a mesh axis runs over, the one named last changes fastest.
Arguments:
- linear_query: bfloat16 [8192, 4096], P('seq', 'tensor'), may hold values from -6 to 6
- linear_key: bfloat16 [8192, 4096], P('seq', 'tensor'), may hold values from -6 to 6
- linear_value: bfloat16 [8192, 4096], P('seq', 'tensor'), may hold values from -200 to 200
- output_gate: bfloat16 [8192, 4096], P('seq', 'tensor'), may hold values from -6 to 6
- log_decay: float32 [8192, 32], P('seq', 'tensor'), may hold values from -0.6 to 0
- softmax_query: bfloat16 [8192, 4096], P('seq', 'tensor'), may hold values from -4.75 to 4.75
- softmax_key: bfloat16 [8192, 4096], P('seq', 'tensor'), may hold values from -4.75 to 4.75
- document_lengths: int32 [8], replicated, may hold values from 1 to 4096, 8192 in all
Outputs:
- linear_mixed: bfloat16 [8192, 4096], P('seq', 'tensor')
- softmax_mixed: bfloat16 [8192, 4096], P('seq', 'tensor')
The draws below stay inside these ranges and needn't reach their ends.
Inputs may be any that keep to these rules, and one draw needn't show every extreme that they name: `document_lengths`: the 8 lengths sum to 8192.
All inputs are finite; a program needn't handle non-finite values.
Results may differ from the reference program's by a relative error of at most 0.0058.
Values may be sent and summed in bfloat16 or wider, within the bound.
A program may use at most 128 MiB of HBM per device.

```python
import math
import jax
import jax.numpy as jnp
import numpy as np
from jax import lax

MIXER_COUNT = 32
HD = 128
BLOCK = 128
DOCS = 8
TOK_DEV = 256
SEQUENCE_ITEMS = 8192


def draw_linear_value(key, part):
    key = jax.random.fold_in(key, 11)
    base_key, row_key = jax.random.split(key)
    head_place = jnp.arange(MIXER_COUNT, dtype=jnp.float32) / (MIXER_COUNT - 1)
    row_scale = jnp.exp(jax.random.uniform(row_key, (SEQUENCE_ITEMS, 1, 1), jnp.float32, 0.0, math.log(10.0)))
    base = jnp.clip(jax.random.normal(base_key, (SEQUENCE_ITEMS, MIXER_COUNT, HD), jnp.float32), -4.0, 4.0)
    head_scale = 10.0 ** head_place
    value = 0.5 * base * head_scale[None, :, None] * row_scale
    return value.reshape(SEQUENCE_ITEMS, MIXER_COUNT * HD).astype(jnp.bfloat16)


def draw_log_decay(key, part):
    key = jax.random.fold_in(key, 23)
    keys = jax.random.split(key, 5)
    fast_share = 0.5
    quick_route = jax.random.bernoulli(keys[0], fast_share, (MIXER_COUNT,))
    rate = jnp.where(quick_route, 1.0 / 40.0, math.log(10.0) / (4.0 * SEQUENCE_ITEMS))
    shards = SEQUENCE_ITEMS // TOK_DEV
    shard_factor = jnp.exp(jax.random.uniform(keys[1], (shards, 1, MIXER_COUNT), jnp.float32, -math.log(2.0), math.log(2.0)))
    token_factor = jax.random.uniform(keys[2], (shards, TOK_DEV, MIXER_COUNT), jnp.float32, 0.5, 1.5)
    smooth = -(rate[None, None, :] * shard_factor * token_factor).reshape(SEQUENCE_ITEMS, MIXER_COUNT)
    third = SEQUENCE_ITEMS // 3
    marked_places = jnp.arange(3, dtype=jnp.int32) * third + jax.random.randint(keys[3], (3,), 0, third)
    objective_scalar = jax.random.uniform(keys[4], (3, MIXER_COUNT), jnp.float32, 0.2, 0.4)
    run_span = jnp.where(quick_route[None, :], 0.0, jnp.log(1.0 - objective_scalar))
    surplus_share = jnp.zeros((SEQUENCE_ITEMS, MIXER_COUNT), jnp.float32).at[marked_places].add(run_span)
    return smooth + surplus_share


def draw_softmax_query(key, part):
    key = jax.random.fold_in(key, 31)
    base = jnp.clip(1.75 * jax.random.normal(key, (SEQUENCE_ITEMS, MIXER_COUNT, HD), jnp.float32), -4.5, 4.5)
    return base.reshape(SEQUENCE_ITEMS, MIXER_COUNT * HD).astype(jnp.bfloat16)


def draw_softmax_key(key, part):
    key = jax.random.fold_in(key, 37)
    base = jnp.clip(1.75 * jax.random.normal(key, (SEQUENCE_ITEMS, MIXER_COUNT, HD), jnp.float32), -4.5, 4.5)
    return base.reshape(SEQUENCE_ITEMS, MIXER_COUNT * HD).astype(jnp.bfloat16)


def block_scale(rng, shape, cuts, low, high):
    level = 1.0
    for position, shards_of in cuts:
        heights = jax.random.uniform(jax.random.fold_in(jax.random.fold_in(rng, 6), position), (shards_of,), jnp.float32, low / len(cuts), high / len(cuts))
        level = level * jnp.repeat(jnp.exp(heights), shape[position] // shards_of).reshape((-1,) + (1,) * (len(shape) - 1 - position))
    return level


def length_profile(number_of, total, most, skew):
    loads = [(1 << 20) // math.isqrt(rank ** skew) + 1 for rank in range(2, number_of + 1)]
    surplus, given = total - most - (number_of - 1), [1] * (number_of - 1)
    while surplus > 0:
        free = [i for i in range(number_of - 1) if given[i] < most]
        mass, left = sum([loads[i] for i in free]), surplus
        for i in free:
            addition = min(most - given[i], max(1, left * loads[i] // mass), surplus)
            given[i] = given[i] + addition
            surplus = surplus - addition
    return np.array([most] + given)


def ragged_sizes(own_key, number_of, total, bound, lean):
    if number_of == 2:
        one = jax.random.randint(own_key, (), max(1, total - bound), min(bound, total - 1) + 1)
        return jnp.stack([one, total - one])
    tallies = jnp.asarray(length_profile(number_of, total, bound, lean), jnp.int32)
    couples = (number_of - 1) // 2
    giver, receiver = tallies[1:1 + 2 * couples:2], tallies[2:2 + 2 * couples:2]
    margin = jnp.minimum(giver - 1, bound - receiver)
    passed = jax.random.randint(jax.random.fold_in(own_key, 1), (couples,), 0, 1 << 20) % (margin + 1)
    tallies = tallies.at[1:1 + 2 * couples:2].set(giver - passed).at[2:2 + 2 * couples:2].set(receiver + passed)
    return tallies[jax.random.permutation(jax.random.fold_in(own_key, 2), number_of)]


def gaussian(key, extent, scale, most, pieces=(), kind=jnp.bfloat16):
    factor_of = block_scale(key, extent, pieces, -0.22, 0.18) if pieces else 1.0
    entries = jax.random.normal(key, extent, jnp.float32) * scale * factor_of
    return jnp.minimum(jnp.maximum(entries, -most), most).astype(kind)


def setup_inputs(seed: int = 0) -> dict:
    splits = jax.random.split(jax.random.key(seed), 9)
    linear_query = gaussian(splits[0], (SEQUENCE_ITEMS, MIXER_COUNT * HD), 1.0, 6.0, ((0, 32), (1, 8)))
    linear_key = gaussian(splits[1], (SEQUENCE_ITEMS, MIXER_COUNT * HD), 1.0, 6.0, ((0, 32), (1, 8)))
    linear_value = draw_linear_value(jax.random.fold_in(splits[8], 71), 0)
    output_gate = gaussian(splits[3], (SEQUENCE_ITEMS, MIXER_COUNT * HD), 1.0, 6.0, ((0, 32), (1, 8)))
    log_decay = draw_log_decay(jax.random.fold_in(splits[8], 71), 0)
    softmax_query = draw_softmax_query(jax.random.fold_in(splits[8], 71), 0)
    softmax_key = draw_softmax_key(jax.random.fold_in(splits[8], 71), 0)
    document_lengths = ragged_sizes(splits[7], DOCS, SEQUENCE_ITEMS, SEQUENCE_ITEMS // 2, 2).astype(jnp.int32)
    return {"linear_query": linear_query, "linear_key": linear_key, "linear_value": linear_value, "output_gate": output_gate, "log_decay": log_decay, "softmax_query": softmax_query, "softmax_key": softmax_key, "document_lengths": document_lengths}


precise = lax.Precision.HIGHEST
floor_score = -1e+30

def segments_of(positions, document_lengths):
    doc_ends = jnp.cumsum(document_lengths).astype(jnp.int32)
    inside = (positions[:, None] >= doc_ends[None, :]).astype(jnp.int32)
    counted = lax.optimization_barrier(jnp.sum(inside, axis=1)).astype(jnp.int32)
    return jnp.where(positions < 0, jnp.int32(-1), counted)

def block_step(state, inputs):
    query_blk, key_blk, value_blk, decay_blk, segment_blk, before_blk = inputs
    running = jnp.cumsum(decay_blk, axis=0)
    kept = (segment_blk == before_blk).astype(jnp.float32)
    leading = jnp.exp(running) * kept[:, None]
    query_wide = query_blk.astype(jnp.float32)
    value_wide = value_blk.astype(jnp.float32)
    carried = jnp.einsum('chd,hde->che', query_wide * leading[:, :, None], state, precision=precise)
    scores = jnp.einsum('chd,jhd->hcj', query_wide, key_blk.astype(jnp.float32))
    count = query_blk.shape[0]
    indices = jnp.arange(count, dtype=jnp.int32)
    allowed = (indices[None, :] <= indices[:, None]) & (segment_blk[None, :] == segment_blk[:, None])
    running_t = running.T
    spread = jnp.where(allowed[None], running_t[:, :, None] - running_t[:, None, :], 0.0)
    weights = jnp.where(allowed[None], jnp.exp(spread), 0.0)
    block_weights = lax.optimization_barrier((scores * weights).astype(jnp.bfloat16)).astype(jnp.float32)
    local_part = jnp.einsum('hcj,jhe->che', block_weights, value_wide)
    final_run = running[-1]
    fade = jnp.where((segment_blk == segment_blk[-1])[:, None], jnp.exp(final_run[None, :] - running), 0.0)
    decayed = (key_blk.astype(jnp.float32) * fade[:, :, None]).astype(jnp.bfloat16)
    decayed = lax.optimization_barrier(decayed).astype(jnp.float32)
    fresh = jnp.einsum('jhd,jhe->hde', decayed, value_wide)
    state = (jnp.exp(final_run) * kept[-1])[:, None, None] * state + fresh
    return (state, carried + local_part)

def lightning_layer(linear_query, linear_key, linear_value, output_gate, log_decay, document_lengths):
    blocks = SEQUENCE_ITEMS // BLOCK
    positions = jnp.arange(SEQUENCE_ITEMS, dtype=jnp.int32)
    segment_ids = segments_of(positions, document_lengths)
    before_ids = segments_of(positions - 1, document_lengths)
    shape = (blocks, BLOCK, MIXER_COUNT, HD)
    inputs = (linear_query.reshape(shape), linear_key.reshape(shape), linear_value.reshape(shape), log_decay.reshape(blocks, BLOCK, MIXER_COUNT), segment_ids.reshape(blocks, BLOCK), before_ids.reshape(blocks, BLOCK)[:, 0])
    state = jnp.zeros((MIXER_COUNT, HD, HD), jnp.float32)
    _, attended = lax.scan(block_step, state, inputs)
    attended = attended.reshape(SEQUENCE_ITEMS, MIXER_COUNT, HD)
    power = lax.optimization_barrier(jnp.sum(attended * attended, axis=(1, 2)))
    scale = lax.rsqrt(power / (MIXER_COUNT * HD) + 1e-06)
    gated = attended.reshape(SEQUENCE_ITEMS, MIXER_COUNT * HD) * scale[:, None] * jax.nn.sigmoid(output_gate.astype(jnp.float32))
    return gated.astype(jnp.bfloat16)

def softmax_layer(softmax_query, softmax_key, values, document_lengths):
    positions = jnp.arange(SEQUENCE_ITEMS, dtype=jnp.int32)
    segment_ids = segments_of(positions, document_lengths)
    row_block = math.gcd(SEQUENCE_ITEMS, 512)

    def heads_first(array):
        return array.reshape(SEQUENCE_ITEMS, MIXER_COUNT, HD).transpose(1, 0, 2)

    def one_head(inputs):
        query_head, key_head, value_head = inputs

        def one_block(index):
            start = index * row_block
            query_rows = lax.dynamic_slice_in_dim(query_head, start, row_block, 0)
            query_pos = start + jnp.arange(row_block, dtype=jnp.int32)
            query_seg = lax.dynamic_slice_in_dim(segment_ids, start, row_block, 0)
            scores = jnp.dot(query_rows, key_head.T, preferred_element_type=jnp.float32) * HD ** (-0.5)
            allowed = (positions[None, :] <= query_pos[:, None]) & (segment_ids[None, :] == query_seg[:, None])
            scores = jnp.where(allowed, scores, floor_score)
            top = lax.optimization_barrier(jnp.max(scores, axis=1, keepdims=True))
            raised = jnp.where(allowed, jnp.exp(scores - top), 0.0)
            denominators = lax.optimization_barrier(jnp.sum(raised, axis=1, keepdims=True))
            probabilities = raised.astype(jnp.bfloat16)
            return jnp.dot(probabilities, value_head, preferred_element_type=jnp.float32) / denominators
        return lax.map(one_block, jnp.arange(SEQUENCE_ITEMS // row_block, dtype=jnp.int32))
    mixed = lax.map(one_head, (heads_first(softmax_query), heads_first(softmax_key), heads_first(values)))
    mixed = mixed.reshape(MIXER_COUNT, SEQUENCE_ITEMS, HD).transpose(1, 0, 2).reshape(SEQUENCE_ITEMS, MIXER_COUNT * HD)
    return mixed.astype(jnp.bfloat16)

def reference(linear_query, linear_key, linear_value, output_gate, log_decay, softmax_query, softmax_key, document_lengths):
    linear_mixed = lightning_layer(linear_query, linear_key, linear_value, output_gate, log_decay, document_lengths)
    softmax_mixed = softmax_layer(softmax_query, softmax_key, linear_mixed, document_lengths)
    return (linear_mixed, softmax_mixed)
```

```python
import functools
import math

import jax
import jax.numpy as jnp
from jax import lax
from jax.experimental import pallas as pl
from jax.experimental.pallas import tpu as pltpu
from jax.sharding import PartitionSpec as P

MESH = pl.DeviceIdType.MESH
HD = 128
DOCS = 8
ROWS = 256
HEADS = 4
SEQ = 32
NZ = 8
NY = 4
WIDTH = HEADS * HD
FLOOR = -1e30
EXPONENT = math.log2(math.e) * HD**-0.5
NEAREST = (0, 1, 7, 2, 6, 3, 5, 4)
F32 = jnp.float32
BF16 = jnp.bfloat16


def mm(a, b, dims, precision=None):
    return lax.dot_general(
        a, b, (dims, ((), ())), preferred_element_type=F32, precision=precision
    )


def iota(shape, dim):
    return lax.broadcasted_iota(jnp.int32, shape, dim)


def doc_start(pos, ends):
    start = jnp.zeros_like(pos)
    for end in ends:
        start = jnp.where(pos >= end, end, start)
    return start


def kernel(
    docs, lq_h, lk_h, lv_h, gate_h, decay_h, sq_h, sk_h,
    mixed_h, out_h,
    lq, lk, lv, gate, decay, decay_pad, att,
    s_send, p1_recv, p2_send, s_in, dec_send, dec_recv, power, mix,
    keys, values, queries, scores, probs, dens, o_send, o_recv,
    load_sem, p1_ss, p1_rs, dec_ss, dec_rs, p2_ss, p2_rs, pw_ss, pw_rs,
    kz_ss, kz_rs, qz_ss, qz_rs, vz_ss, vz_rs,
    ky_ss, ky_rs, kd_ss, kd_rs, vy_ss, vy_rs, vd_ss, vd_rs, o_ss, o_rs, out_sem,
):
    s = lax.axis_index("seq")
    t = lax.axis_index("tensor")
    z, y, x, c = s // NY, s % NY, t // 2, t % 2
    sib = 2 * x + (1 - c)

    barrier = pltpu.get_barrier_semaphore()
    partners = [((s + k) % SEQ, t) for k in range(1, SEQ)]
    partners += [(((z + k) % NZ) * NY + y, sib) for k in range(NZ)]
    partners += [(s, (2 * x + 2 * k + cc) % 8) for k in range(1, 4) for cc in range(2)]
    loads = []
    for n, (src, dst) in enumerate(
        ((decay_h, decay), (lk_h, lk), (lv_h, lv), (lq_h, lq), (gate_h, gate))
    ):
        cp = pltpu.make_async_copy(src, dst, load_sem.at[n])
        cp.start()
        loads.append(cp)
    for dev in partners:
        pl.semaphore_signal(barrier, inc=1, device_id=dev, device_id_type=MESH)

    pending = []

    def remote(src, dst, ss, rs, dev):
        cp = pltpu.make_async_remote_copy(
            src_ref=src, dst_ref=dst, send_sem=ss, recv_sem=rs, device_id=dev, device_id_type=MESH
        )
        return cp

    def send(src, dst, ss, rs, dev):
        cp = remote(src, dst, ss, rs, dev)
        cp.start()
        pending.append((cp, None))

    def send_or_keep(here, src, dst, ss, rs, dev):
        cp = remote(src, dst, ss, rs, dev)

        @pl.when(jnp.logical_not(here))
        def _():
            cp.start()

        @pl.when(here)
        def _():
            pltpu.make_async_copy(src, dst, rs).start()

        pending.append((cp, here))

    def arrived(dst, rs):
        pltpu.make_async_copy(dst, dst, rs).wait()

    ends = []
    total = jnp.int32(0)
    for d in range(DOCS):
        total = total + docs[d]
        ends.append(total)
    first = s * ROWS
    pos = first + iota((ROWS, 1), 0)
    start = doc_start(pos, ends)
    last_start = doc_start(first + ROWS - 1, ends)
    kept = (start < first).astype(F32)
    in_last = pos >= last_start

    loads[0].wait()
    decay_pad[...] = jnp.zeros_like(decay_pad)
    decay_pad[:, 0:HEADS] = decay[...]
    lower = (iota((ROWS, ROWS), 1) <= iota((ROWS, ROWS), 0)).astype(F32)
    running = mm(lower, decay_pad[...], ((1,), (0,)), lax.Precision.HIGHEST)
    final = running[ROWS - 1 : ROWS, :]
    fade = jnp.where(in_last, jnp.exp(jnp.minimum(final - running, 0.0)), 0.0)
    whole = jnp.where(last_start < first, jnp.exp(final), 0.0)
    for h in range(HEADS):
        dec_send[h] = jnp.broadcast_to(whole[:, h : h + 1], (1, HD))
    loads[1].wait()
    loads[2].wait()
    for h in range(HEADS):
        cols = slice(h * HD, (h + 1) * HD)
        faded = (lk[:, cols].astype(F32) * fade[:, h : h + 1]).astype(BF16)
        s_send[h * HD : (h + 1) * HD, :] = mm(faded, lv[:, cols], ((0,), (0,))).astype(BF16)

    pl.semaphore_wait(barrier, len(partners))

    piece = 16
    order = [k for pair in zip(range(1, 17), range(31, 15, -1)) for k in pair]
    order = list(dict.fromkeys(order))
    for k in order:
        p = (s + k) % SEQ
        send(dec_send.at[p // 8], dec_recv.at[s], dec_ss.at[k], dec_rs.at[k], (p, t))
        send(
            s_send.at[pl.ds(pl.multiple_of(p * piece, piece), piece)],
            p1_recv.at[s], p1_ss.at[k], p1_rs.at[k], (p, t),
        )
    dec_recv[s] = dec_send[s // 8]
    p1_recv[s] = s_send[pl.ds(pl.multiple_of(s * piece, piece), piece), :]

    def to_heads(src, dst, ss, rs):
        for i in range(HEADS):
            for blk in range(2):
                zz = HEADS * c + i
                here = jnp.logical_and(zz == z, blk == c)
                send_or_keep(
                    here,
                    src.at[pl.ds(blk * HD, HD), pl.ds(i * HD, HD)],
                    dst(blk), ss.at[2 * i + blk], rs.at[z],
                    (zz * NY + y, 2 * x + blk),
                )

    to_heads(sk_h, lambda blk: keys.at[z, 2 * y + blk], kz_ss, kz_rs)
    to_heads(sq_h, lambda blk: queries.at[z], qz_ss, qz_rs)

    loads[3].wait()
    lead = jnp.exp(running) * kept
    running_t = running.T
    col = iota((1, ROWS), 1)
    allowed = (col <= iota((ROWS, 1), 0)) & (first + col >= start)
    for h in range(HEADS):
        cols = slice(h * HD, (h + 1) * HD)
        dots = mm(lq[:, cols], lk[:, cols], ((1,), (1,)))
        spread = jnp.where(allowed, running[:, h : h + 1] - running_t[h : h + 1, :], 0.0)
        weights = jnp.where(allowed, dots * jnp.exp(spread), 0.0).astype(BF16)
        att[:, cols] = mm(weights, lv[:, cols], ((1,), (0,)))

    for k in order:
        src = (s + SEQ - k) % SEQ
        arrived(dec_recv.at[src], dec_rs.at[k])
        arrived(p1_recv.at[src], p1_rs.at[k])
    state = jnp.zeros((piece, HD), F32)
    for r in range(SEQ):
        p2_send[r] = state.astype(BF16)
        state = dec_recv[r] * state + p1_recv[r].astype(F32)
    for k in order:
        p = (s + k) % SEQ
        send(p2_send.at[p], s_in.at[s], p2_ss.at[k], p2_rs.at[k], (p, t))
    s_in[s] = p2_send[s]

    mine = 2 * y + c
    for k in NEAREST:
        zz = (z + k) % NZ
        arrived(keys.at[zz, mine], kz_rs.at[zz])
    for k in (1, 3, 2):
        send(
            keys.at[:, mine], keys.at[:, mine], ky_ss.at[k], ky_rs.at[k],
            (z * NY + (y + k) % NY, t),
        )
    send(keys.at[:, mine], keys.at[:, mine], kd_ss.at[0], kd_rs.at[0], (s, sib))

    for k in order:
        src = (s + SEQ - k) % SEQ
        arrived(s_in.at[src], p2_rs.at[k])
    loads[4].wait()
    power_col = jnp.zeros((ROWS, 1), F32)
    for h in range(HEADS):
        cols = slice(h * HD, (h + 1) * HD)
        state_h = s_in[h * 8 : (h + 1) * 8].reshape(HD, HD)
        carried = mm(lq[:, cols], state_h, ((1,), (0,)))
        full = att[:, cols] + lead[:, h : h + 1] * carried
        att[:, cols] = full
        power_col = power_col + jnp.sum(full * full, axis=1, keepdims=True)
    diag = iota((ROWS, ROWS), 0) == iota((ROWS, ROWS), 1)
    power[t] = jnp.sum(jnp.where(diag, power_col, 0.0), axis=0, keepdims=True)
    for k in range(1, 8):
        send(power.at[t], power.at[t], pw_ss.at[k], pw_rs.at[k], (s, (t + k) % 8))
    for h in range(HEADS):
        cols = slice(h * HD, (h + 1) * HD)
        att[:, cols] = att[:, cols] * jax.nn.sigmoid(gate[:, cols].astype(F32))
    for k in range(1, 8):
        arrived(power.at[(t + 8 - k) % 8], pw_rs.at[k])
    total_row = power[0]
    for k in range(1, 8):
        total_row = total_row + power[k]
    scale_row = lax.rsqrt(total_row / (32 * HD) + 1e-06)
    scale = jnp.sum(jnp.where(diag, scale_row, 0.0), axis=1, keepdims=True)
    for h in range(HEADS):
        cols = slice(h * HD, (h + 1) * HD)
        mix[:, cols] = (att[:, cols] * scale).astype(BF16)
    to_heads(mix, lambda blk: values.at[z, 2 * y + blk], vz_ss, vz_rs)
    mixed_copy = pltpu.make_async_copy(mix, mixed_h, out_sem.at[0])
    mixed_copy.start()

    def spread_values(k):
        zz = (z + k) % NZ
        arrived(values.at[zz, mine], vz_rs.at[zz])
        for d in (1, 3, 2):
            send(
                values.at[zz, mine], values.at[zz, mine],
                vy_ss.at[k, d], vy_rs.at[zz, d], (z * NY + (y + d) % NY, t),
            )
        send(values.at[zz, mine], values.at[zz, mine], vd_ss.at[k, 0], vd_rs.at[zz, 0], (s, sib))

    def pass_values(k):
        zz = (z + k) % NZ
        for d in (1, 3, 2):
            block = 2 * ((y + NY - d) % NY) + c
            arrived(values.at[zz, block], vy_rs.at[zz, d])
            send(
                values.at[zz, block], values.at[zz, block],
                vd_ss.at[k, d], vd_rs.at[zz, d], (s, sib),
            )

    def finish_values(k):
        zz = (z + k) % NZ
        for d in range(NY):
            block = 2 * ((y + NY - d) % NY) + (1 - c)
            arrived(values.at[zz, block], vd_rs.at[zz, d])

    for k in (1, 3, 2):
        block = 2 * ((y + NY - k) % NY) + c
        arrived(keys.at[:, block], ky_rs.at[k])
        send(keys.at[:, block], keys.at[:, block], kd_ss.at[k], kd_rs.at[k], (s, sib))
    for zz in range(NZ):
        arrived(queries.at[zz], qz_rs.at[zz])
    for k in range(NY):
        block = 2 * ((y + NY - k) % NY) + (1 - c)
        arrived(keys.at[:, block], kd_rs.at[k])

    def softmax_tile(zt):
        low = max(zt - 4, 0)
        chunks = 2 * (zt - low + 1)
        q = queries[zt]
        i = zt * 1024 + y * ROWS + c * HD + iota((HD, 1), 0)
        i_start = doc_start(i, ends)

        def first_pass(g, top):
            block = keys[low + g // 2, pl.ds((g % 2) * 4, 4)].reshape(512, HD)
            dots = mm(q, block, ((1,), (1,)))
            j = low * 1024 + g * 512 + iota((1, 512), 1)
            dots = jnp.where((j <= i) & (j >= i_start), dots, FLOOR)
            scores[:, pl.ds(pl.multiple_of(g * 512, 512), 512)] = dots
            for n in range(4):
                top = jnp.maximum(top, dots[:, n * HD : (n + 1) * HD])
            return top

        top = lax.fori_loop(0, chunks, first_pass, jnp.full((HD, HD), FLOOR, F32))
        top = jnp.max(top, axis=1, keepdims=True)

        def second_pass(g, den):
            at = pl.ds(pl.multiple_of(g * 512, 512), 512)
            raised = jnp.exp2((scores[:, at] - top) * EXPONENT)
            probs[zt, :, at] = raised.astype(BF16)
            for n in range(4):
                den = den + raised[:, n * HD : (n + 1) * HD]
            return den

        den = lax.fori_loop(0, chunks, second_pass, jnp.zeros((HD, HD), F32))
        dens[zt] = jnp.broadcast_to(jnp.sum(den, axis=1, keepdims=True), (HD, HD))

    spread_values(0)
    softmax_tile(0)
    softmax_tile(1)
    spread_values(1)
    spread_values(7)
    softmax_tile(2)
    spread_values(2)
    spread_values(6)
    softmax_tile(3)
    spread_values(3)
    spread_values(5)
    spread_values(4)
    softmax_tile(4)
    pass_values(0)
    pass_values(1)
    pass_values(7)
    softmax_tile(5)
    pass_values(2)
    pass_values(6)
    softmax_tile(6)
    pass_values(3)
    pass_values(5)
    softmax_tile(7)
    pass_values(4)
    for k in NEAREST:
        finish_values(k)

    for zt in range(NZ):
        low = max(zt - 4, 0)

        def weigh(g, acc):
            at = pl.ds(pl.multiple_of(g * 1024, 1024), 1024)
            return acc + mm(
                probs[zt, :, at], values[low + g].reshape(1024, HD), ((1,), (0,))
            )

        acc = lax.fori_loop(0, zt - low + 1, weigh, jnp.zeros((HD, HD), F32))
        o_send[zt] = (acc / dens[zt]).astype(BF16)
        here = jnp.logical_and(z == zt, z // HEADS == c)
        send_or_keep(
            here, o_send.at[zt],
            o_recv.at[pl.ds(pl.multiple_of(c * HD, HD), HD), pl.ds(pl.multiple_of((z % HEADS) * HD, HD), HD)],
            o_ss.at[zt], o_rs.at[2 * (z % HEADS) + c],
            (zt * NY + y, 2 * x + z // HEADS),
        )
    for i in range(HEADS):
        for blk in range(2):
            arrived(
                o_recv.at[pl.ds(blk * HD, HD), pl.ds(i * HD, HD)], o_rs.at[2 * i + blk]
            )
    out_copy = pltpu.make_async_copy(o_recv, out_h, out_sem.at[1])
    out_copy.start()
    for cp, here in pending:
        if here is None:
            cp.wait_send()
        else:
            pl.when(jnp.logical_not(here))(cp.wait_send)
    mixed_copy.wait()
    out_copy.wait()


def on_device(lq, lk, lv, gate, decay, sq, sk, docs):
    dma = pltpu.SemaphoreType.DMA
    vmem = pltpu.VMEM
    return pl.pallas_call(
        kernel,
        out_shape=(
            jax.ShapeDtypeStruct((ROWS, WIDTH), BF16),
            jax.ShapeDtypeStruct((ROWS, WIDTH), BF16),
        ),
        in_specs=[pl.BlockSpec(memory_space=pltpu.SMEM)] + [pl.BlockSpec(memory_space=pl.ANY)] * 7,
        out_specs=(pl.BlockSpec(memory_space=pl.ANY), pl.BlockSpec(memory_space=pl.ANY)),
        scratch_shapes=[
            vmem((ROWS, WIDTH), BF16), vmem((ROWS, WIDTH), BF16),
            vmem((ROWS, WIDTH), BF16), vmem((ROWS, WIDTH), BF16),
            vmem((ROWS, HEADS), F32), vmem((ROWS, HD), F32), vmem((ROWS, WIDTH), F32),
            vmem((WIDTH, HD), BF16), vmem((SEQ, 16, HD), BF16),
            vmem((SEQ, 16, HD), BF16), vmem((SEQ, 16, HD), BF16),
            vmem((HEADS, 1, HD), F32), vmem((SEQ, 1, HD), F32),
            vmem((8, 1, ROWS), F32), vmem((ROWS, WIDTH), BF16),
            vmem((NZ, 8, HD, HD), BF16), vmem((NZ, 8, HD, HD), BF16),
            vmem((NZ, HD, HD), BF16), vmem((HD, 5 * 1024), F32),
            vmem((NZ, HD, 5 * 1024), BF16), vmem((NZ, HD, HD), F32),
            vmem((NZ, HD, HD), BF16), vmem((ROWS, WIDTH), BF16),
            dma((5,)), dma((SEQ,)), dma((SEQ,)), dma((SEQ,)), dma((SEQ,)),
            dma((SEQ,)), dma((SEQ,)), dma((8,)), dma((8,)),
            dma((8,)), dma((8,)), dma((8,)), dma((8,)), dma((8,)), dma((8,)),
            dma((4,)), dma((4,)), dma((4,)), dma((4,)),
            dma((8, 4)), dma((8, 4)), dma((8, 4)), dma((8, 4)),
            dma((8,)), dma((8,)), dma((2,)),
        ],
        compiler_params=pltpu.CompilerParams(
            collective_id=0, has_side_effects=True, vmem_limit_bytes=48 << 20
        ),
    )(docs, lq, lk, lv, gate, decay, sq, sk)


def solution(mesh):
    split = P("seq", "tensor")
    return jax.shard_map(
        on_device,
        mesh=mesh,
        in_specs=(split,) * 7 + (P(),),
        out_specs=(split, split),
        check_vma=False,
    )
```

```python
import functools
import math

import jax
import jax.numpy as jnp
from jax import lax
from jax.experimental import pallas as pl
from jax.experimental.pallas import tpu as pltpu
from jax.sharding import PartitionSpec as P

MESH = pl.DeviceIdType.MESH
HD = 128
DOCS = 8
ROWS = 256
HEADS = 4
SEQ = 32
NZ = 8
NY = 4
WIDTH = HEADS * HD
FLOOR = -1e30
EXPONENT = math.log2(math.e) * HD**-0.5
NEAREST = (0, 1, 7, 2, 6, 3, 5, 4)
F32 = jnp.float32
BF16 = jnp.bfloat16


def mm(a, b, dims, precision=None):
    return lax.dot_general(
        a, b, (dims, ((), ())), preferred_element_type=F32, precision=precision
    )


def iota(shape, dim):
    return lax.broadcasted_iota(jnp.int32, shape, dim)


def doc_start(pos, ends):
    start = jnp.zeros_like(pos)
    for end in ends:
        start = jnp.where(pos >= end, end, start)
    return start


def kernel(
    docs, lq_h, lk_h, lv_h, gate_h, decay_h, sq_h, sk_h,
    mixed_h, out_h,
    lq, lk, lv, gate, decay, att,
    s_send, p1_recv, p2_send, s_in, dec_send, dec_recv, power, mix, plain, scales, acc,
    keys, values, queries, scores, probs, dens, o_send, o_recv,
    load_sem, p1_ss, p1_rs, dec_ss, dec_rs, p2_ss, p2_rs, pw_ss, pw_rs,
    kz_ss, kz_rs, qz_ss, qz_rs, vz_ss, vz_rs,
    ky_ss, ky_rs, kd_ss, kd_rs, vy_ss, vy_rs, vd_ss, vd_rs, sc_ss, sc_rs, o_ss, o_rs, out_sem,
):
    s = lax.axis_index("seq")
    t = lax.axis_index("tensor")
    z, y, x, c = s // NY, s % NY, t // 2, t % 2
    sib = 2 * x + (1 - c)

    barrier = pltpu.get_barrier_semaphore()
    partners = [((s + k) % SEQ, t) for k in range(1, SEQ)]
    partners += [(((z + k) % NZ) * NY + y, sib) for k in range(NZ)]
    partners += [(s, (2 * x + 2 * k + cc) % 8) for k in range(1, 4) for cc in range(2)]
    loads = []
    for n, (src, dst) in enumerate(
        ((decay_h, decay), (lk_h, lk), (lv_h, lv), (lq_h, lq), (gate_h, gate))
    ):
        cp = pltpu.make_async_copy(src, dst, load_sem.at[n])
        cp.start()
        loads.append(cp)
    for dev in partners:
        pl.semaphore_signal(barrier, inc=1, device_id=dev, device_id_type=MESH)

    pending = []

    def remote(src, dst, ss, rs, dev):
        cp = pltpu.make_async_remote_copy(
            src_ref=src, dst_ref=dst, send_sem=ss, recv_sem=rs, device_id=dev, device_id_type=MESH
        )
        return cp

    def send(src, dst, ss, rs, dev):
        cp = remote(src, dst, ss, rs, dev)
        cp.start()
        pending.append((cp, None))

    def send_or_keep(here, src, dst, ss, rs, dev):
        cp = remote(src, dst, ss, rs, dev)

        @pl.when(jnp.logical_not(here))
        def _():
            cp.start()

        @pl.when(here)
        def _():
            pltpu.make_async_copy(src, dst, rs).start()

        pending.append((cp, here))

    def arrived(dst, rs):
        pltpu.make_async_copy(dst, dst, rs).wait()

    ends = []
    total = jnp.int32(0)
    for d in range(DOCS):
        total = total + docs[d]
        ends.append(total)
    first = s * ROWS
    pos = first + iota((ROWS, 1), 0)
    start = doc_start(pos, ends)
    last_start = doc_start(first + ROWS - 1, ends)
    kept = (start < first).astype(F32)
    in_last = pos >= last_start

    loads[0].wait()
    lower = (iota((ROWS, ROWS), 1) <= iota((ROWS, ROWS), 0)).astype(BF16)
    rest = decay[...]
    running = jnp.zeros((ROWS, HEADS), F32)
    running_t = jnp.zeros((HEADS, ROWS), F32)
    for _ in range(3):
        part = rest.astype(BF16)
        rest = rest - part.astype(F32)
        running = running + mm(lower, part, ((1,), (1,)))
        running_t = running_t + mm(part, lower, ((1,), (1,)))
    final = running[ROWS - 1 : ROWS, :]
    fade = jnp.where(in_last, jnp.exp(jnp.minimum(final - running, 0.0)), 0.0)
    whole = jnp.where(last_start < first, jnp.exp(final), 0.0)
    for h in range(HEADS):
        dec_send[h] = jnp.broadcast_to(whole[:, h : h + 1], (1, HD))
    loads[1].wait()
    loads[2].wait()
    for h in range(HEADS):
        cols = slice(h * HD, (h + 1) * HD)
        faded = (lk[:, cols].astype(F32) * fade[:, h : h + 1]).astype(BF16)
        s_send[h * HD : (h + 1) * HD, :] = mm(faded, lv[:, cols], ((0,), (0,))).astype(BF16)

    pl.semaphore_wait(barrier, len(partners))

    piece = 16
    order = sorted(
        range(1, SEQ),
        key=lambda k: -min(k // NY, NZ - k // NY) - min(k % NY, NY - k % NY),
    )

    def ahead(k):
        return (z + k // NY) % NZ * NY + (y + k % NY) % NY

    def behind(k):
        return (z + NZ - k // NY) % NZ * NY + (y + NY - k % NY) % NY

    for k in order:
        p = ahead(k)
        send(dec_send.at[p // 8], dec_recv.at[s], dec_ss.at[k], dec_rs.at[k], (p, t))
        send(
            s_send.at[pl.ds(pl.multiple_of(p * piece, piece), piece)],
            p1_recv.at[s], p1_ss.at[k], p1_rs.at[k], (p, t),
        )
    dec_recv[s] = dec_send[s // 8]
    p1_recv[s] = s_send[pl.ds(pl.multiple_of(s * piece, piece), piece), :]

    def to_heads(src, dst, ss, rs):
        for n in range(HEADS):
            i = (z + n + 1) % HEADS
            for blk in range(2):
                zz = HEADS * c + i
                here = jnp.logical_and(zz == z, blk == c)
                send_or_keep(
                    here,
                    src.at[pl.ds(blk * HD, HD), pl.ds(pl.multiple_of(i * HD, HD), HD)],
                    dst(blk), ss.at[2 * n + blk], rs.at[z],
                    (zz * NY + y, 2 * x + blk),
                )

    to_heads(sk_h, lambda blk: keys.at[z, 2 * y + blk], kz_ss, kz_rs)

    loads[3].wait()
    lead = jnp.exp(running) * kept
    col = iota((1, ROWS), 1)
    allowed = (col <= iota((ROWS, 1), 0)) & (first + col >= start)
    for h in range(HEADS):
        cols = slice(h * HD, (h + 1) * HD)
        dots = mm(lq[:, cols], lk[:, cols], ((1,), (1,)))
        spread = jnp.where(allowed, running[:, h : h + 1] - running_t[h : h + 1, :], 0.0)
        weights = jnp.where(allowed, dots * jnp.exp(spread), 0.0).astype(BF16)
        att[:, cols] = mm(weights, lv[:, cols], ((1,), (0,)))

    for k in order:
        src = behind(k)
        arrived(dec_recv.at[src], dec_rs.at[k])
        arrived(p1_recv.at[src], p1_rs.at[k])
    state = jnp.zeros((piece, HD), F32)
    for r in range(SEQ):
        p2_send[r] = state.astype(BF16)
        state = dec_recv[r] * state + p1_recv[r].astype(F32)
    for k in order:
        p = ahead(k)
        send(p2_send.at[p], s_in.at[s], p2_ss.at[k], p2_rs.at[k], (p, t))
    s_in[s] = p2_send[s]
    to_heads(sq_h, lambda blk: queries.at[z], qz_ss, qz_rs)

    mine = 2 * y + c
    for k in NEAREST:
        zz = (z + k) % NZ
        arrived(keys.at[zz, mine], kz_rs.at[zz])
    for k in (1, 3, 2):
        send(
            keys.at[:, mine], keys.at[:, mine], ky_ss.at[k], ky_rs.at[k],
            (z * NY + (y + k) % NY, t),
        )
    send(keys.at[:, mine], keys.at[:, mine], kd_ss.at[0], kd_rs.at[0], (s, sib))

    for k in order:
        src = behind(k)
        arrived(s_in.at[src], p2_rs.at[k])
    loads[4].wait()
    power_col = jnp.zeros((ROWS, 1), F32)
    for h in range(HEADS):
        cols = slice(h * HD, (h + 1) * HD)
        state_h = s_in[h * 8 : (h + 1) * 8].reshape(HD, HD)
        carried = mm(lq[:, cols], state_h, ((1,), (0,)))
        full = att[:, cols] + lead[:, h : h + 1] * carried
        att[:, cols] = full
        power_col = power_col + jnp.sum(full * full, axis=1, keepdims=True)
    diag = iota((ROWS, ROWS), 0) == iota((ROWS, ROWS), 1)
    power[t] = jnp.sum(jnp.where(diag, power_col, 0.0), axis=0, keepdims=True)
    for k in range(1, 8):
        send(power.at[t], power.at[t], pw_ss.at[k], pw_rs.at[k], (s, (t + k) % 8))
    for h in range(HEADS):
        cols = slice(h * HD, (h + 1) * HD)
        gated = att[:, cols] * jax.nn.sigmoid(gate[:, cols].astype(F32))
        att[:, cols] = gated
        plain[:, cols] = gated.astype(BF16)
    to_heads(plain, lambda blk: values.at[z, 2 * y + blk], vz_ss, vz_rs)

    def spread_values(k):
        zz = (z + k) % NZ
        arrived(values.at[zz, mine], vz_rs.at[zz])
        for d in (2, 1, 3):
            send(
                values.at[zz, mine], values.at[zz, mine],
                vy_ss.at[k, d], vy_rs.at[zz, d], (z * NY + (y + d) % NY, t),
            )
        send(values.at[zz, mine], values.at[zz, mine], vd_ss.at[k, 0], vd_rs.at[zz, 0], (s, sib))

    def pass_values(k):
        zz = (z + k) % NZ
        for d in (1, 3, 2):
            block = 2 * ((y + NY - d) % NY) + c
            arrived(values.at[zz, block], vy_rs.at[zz, d])
            send(
                values.at[zz, block], values.at[zz, block],
                vd_ss.at[k, d], vd_rs.at[zz, d], (s, sib),
            )

    def finish_values(k):
        zz = (z + k) % NZ
        for d in range(NY):
            block = 2 * ((y + NY - d) % NY) + (1 - c)
            arrived(values.at[zz, block], vd_rs.at[zz, d])

    def weigh(k):
        zz = (z + k) % NZ

        def add(tiles):
            part = mm(
                probs[zz, 0:tiles].reshape(tiles * HD, 1024),
                values[zz].reshape(1024, HD), ((1,), (0,)),
            )
            at = pl.ds(zz, tiles)
            acc[at] = acc[at] + part.reshape(tiles, HD, HD)

        pl.when(zz < 4)(lambda: add(5))
        pl.when(zz >= 4)(lambda: add(4))

    lane = iota((HD, HD), 1)

    def first_tile(zt):
        q = queries[zt]
        i = zt * 1024 + y * ROWS + c * HD + iota((HD, 1), 0)
        from_start = lane - doc_start(i, ends)
        from_self = lane - i

        def group(m, top, causal):
            block = keys[zt - m].reshape(1024, HD)
            for n in range(4):
                dots = mm(q, block[n * 256 : (n + 1) * 256], ((1,), (1,)))
                for half in range(2):
                    base = (zt - m) * 1024 + n * 256 + half * HD
                    allowed = from_start >= -base
                    if causal:
                        allowed = allowed & (from_self <= -base)
                    at = slice(half * HD, (half + 1) * HD)
                    part = jnp.where(allowed, dots[:, at], FLOOR)
                    scores[zt, m, :, n * 256 + half * HD : n * 256 + (half + 1) * HD] = part
                    top = jnp.maximum(top, part)
            return top

        top = group(0, jnp.full((HD, HD), FLOOR, F32), True)
        top = lax.fori_loop(1, min(zt, 4) + 1, lambda m, v: group(m, v, False), top)
        dens[zt] = jnp.broadcast_to(jnp.max(top, axis=1, keepdims=True), (HD, HD))

    def second_tile(zt):
        top = dens[zt]

        def group(m, den):
            for n in range(8):
                at = slice(n * HD, (n + 1) * HD)
                raised = jnp.exp2((scores[zt, m, :, at] - top) * EXPONENT)
                den = den + raised
                row = scales[(zt - m) * 4 + n // 2][:, (n % 2) * HD : (n % 2 + 1) * HD]
                probs[zt - m, m, :, at] = (raised * row).astype(BF16)
            return den

        den = lax.fori_loop(0, min(zt, 4) + 1, group, jnp.zeros((HD, HD), F32))
        dens[zt] = jnp.broadcast_to(jnp.sum(den, axis=1, keepdims=True), (HD, HD))

    acc[...] = jnp.zeros_like(acc)
    spread_values(0)
    spread_values(1)
    spread_values(7)
    for k in range(1, 8):
        arrived(power.at[(t + 8 - k) % 8], pw_rs.at[k])
    total_row = power[0]
    for k in range(1, 8):
        total_row = total_row + power[k]
    scale_row = lax.rsqrt(total_row / (32 * HD) + 1e-06)
    scales[s] = scale_row
    for k in order:
        send(scales.at[s], scales.at[s], sc_ss.at[k], sc_rs.at[k], (ahead(k), t))
    spread_values(2)
    spread_values(6)
    scale = jnp.sum(jnp.where(diag, scale_row, 0.0), axis=1, keepdims=True)
    for h in range(HEADS):
        cols = slice(h * HD, (h + 1) * HD)
        mix[:, cols] = (att[:, cols] * scale).astype(BF16)
    mixed_copy = pltpu.make_async_copy(mix, mixed_h, out_sem.at[0])
    mixed_copy.start()
    spread_values(3)
    spread_values(5)
    spread_values(4)

    for k in (1, 3, 2):
        block = 2 * ((y + NY - k) % NY) + c
        arrived(keys.at[:, block], ky_rs.at[k])
        send(keys.at[:, block], keys.at[:, block], kd_ss.at[k], kd_rs.at[k], (s, sib))
    for zz in range(NZ):
        arrived(queries.at[zz], qz_rs.at[zz])
    for k in range(NY):
        block = 2 * ((y + NY - k) % NY) + (1 - c)
        arrived(keys.at[:, block], kd_rs.at[k])
    for zt in range(5):
        first_tile(zt)
    pass_values(0)
    pass_values(1)
    first_tile(5)
    first_tile(6)
    pass_values(7)
    first_tile(7)
    for k in order:
        arrived(scales.at[behind(k)], sc_rs.at[k])
    for zt in range(4):
        second_tile(zt)
    pass_values(2)
    second_tile(4)
    pass_values(6)
    second_tile(5)
    pass_values(3)
    second_tile(6)
    pass_values(5)
    second_tile(7)
    for k in NEAREST[:5]:
        finish_values(k)
        weigh(k)
    pass_values(4)
    for k in NEAREST[5:]:
        finish_values(k)
        weigh(k)

    for k in reversed(NEAREST):
        zt = (z + k) % NZ
        o_send[zt] = (acc[zt] / dens[zt]).astype(BF16)
        src = o_send.at[zt]
        dst = o_recv.at[
            pl.ds(pl.multiple_of(c * HD, HD), HD),
            pl.ds(pl.multiple_of((z % HEADS) * HD, HD), HD),
        ]
        rs = o_rs.at[2 * (z % HEADS) + c]
        dev = (zt * NY + y, 2 * x + z // HEADS)
        if k:
            send(src, dst, o_ss.at[k], rs, dev)
        else:
            send_or_keep(z // HEADS == c, src, dst, o_ss.at[k], rs, dev)
    for i in range(HEADS):
        for blk in range(2):
            arrived(
                o_recv.at[pl.ds(blk * HD, HD), pl.ds(i * HD, HD)], o_rs.at[2 * i + blk]
            )
    out_copy = pltpu.make_async_copy(o_recv, out_h, out_sem.at[1])
    out_copy.start()
    for cp, here in pending:
        if here is None:
            cp.wait_send()
        else:
            pl.when(jnp.logical_not(here))(cp.wait_send)
    mixed_copy.wait()
    out_copy.wait()


def on_device(lq, lk, lv, gate, decay, sq, sk, docs):
    dma = pltpu.SemaphoreType.DMA
    vmem = pltpu.VMEM
    return pl.pallas_call(
        kernel,
        out_shape=(
            jax.ShapeDtypeStruct((ROWS, WIDTH), BF16),
            jax.ShapeDtypeStruct((ROWS, WIDTH), BF16),
        ),
        in_specs=[pl.BlockSpec(memory_space=pltpu.SMEM)] + [pl.BlockSpec(memory_space=pltpu.HBM)] * 7,
        out_specs=(pl.BlockSpec(memory_space=pltpu.HBM), pl.BlockSpec(memory_space=pltpu.HBM)),
        scratch_shapes=[
            vmem((ROWS, WIDTH), BF16), vmem((ROWS, WIDTH), BF16),
            vmem((ROWS, WIDTH), BF16), vmem((ROWS, WIDTH), BF16),
            vmem((HEADS, ROWS), F32), vmem((ROWS, WIDTH), F32),
            vmem((WIDTH, HD), BF16), vmem((SEQ, 16, HD), BF16),
            vmem((SEQ, 16, HD), BF16), vmem((SEQ, 16, HD), BF16),
            vmem((HEADS, 1, HD), F32), vmem((SEQ, 1, HD), F32),
            vmem((8, 1, ROWS), F32), vmem((ROWS, WIDTH), BF16), vmem((ROWS, WIDTH), BF16),
            vmem((SEQ, 1, ROWS), F32), vmem((NZ + 3, HD, HD), F32),
            vmem((NZ, 8, HD, HD), BF16), vmem((NZ, 8, HD, HD), BF16),
            vmem((NZ, HD, HD), BF16), vmem((NZ, 5, HD, 1024), F32),
            vmem((NZ, 5, HD, 1024), BF16), vmem((NZ, HD, HD), F32),
            vmem((NZ, HD, HD), BF16), vmem((ROWS, WIDTH), BF16),
            dma((5,)), dma((SEQ,)), dma((SEQ,)), dma((SEQ,)), dma((SEQ,)),
            dma((SEQ,)), dma((SEQ,)), dma((8,)), dma((8,)),
            dma((8,)), dma((8,)), dma((8,)), dma((8,)), dma((8,)), dma((8,)),
            dma((4,)), dma((4,)), dma((4,)), dma((4,)),
            dma((8, 4)), dma((8, 4)), dma((8, 4)), dma((8, 4)),
            dma((SEQ,)), dma((SEQ,)), dma((8,)), dma((8,)), dma((2,)),
        ],
        compiler_params=pltpu.CompilerParams(
            collective_id=0, has_side_effects=True, vmem_limit_bytes=(64 << 20) - (64 << 10)
        ),
    )(docs, lq, lk, lv, gate, decay.T, sq, sk)


def solution(mesh):
    split = P("seq", "tensor")
    return jax.shard_map(
        on_device,
        mesh=mesh,
        in_specs=(split,) * 7 + (P(),),
        out_specs=(split, split),
        check_vma=False,
    )
```

```python
import functools
import math

import jax
import jax.numpy as jnp
from jax import lax
from jax.experimental import pallas as pl
from jax.experimental.pallas import tpu as pltpu
from jax.sharding import PartitionSpec as P

MESH = pl.DeviceIdType.MESH
HD = 128
DOCS = 8
ROWS = 256
HEADS = 4
SEQ = 32
NZ = 8
NY = 4
WIDTH = HEADS * HD
FLOOR = -1e30
EXPONENT = math.log2(math.e) * HD**-0.5
NEAREST = (0, 1, 7, 2, 6, 3, 5, 4)
F32 = jnp.float32
BF16 = jnp.bfloat16


def mm(a, b, dims, precision=None):
    return lax.dot_general(
        a, b, (dims, ((), ())), preferred_element_type=F32, precision=precision
    )


def iota(shape, dim):
    return lax.broadcasted_iota(jnp.int32, shape, dim)


def doc_start(pos, ends):
    start = jnp.zeros_like(pos)
    for end in ends:
        start = jnp.where(pos >= end, end, start)
    return start


def kernel(
    docs, lq_h, lk_h, lv_h, gate_h, decay_h, sq_h, sk_h,
    mixed_h, out_h,
    lq, lk, lv, gate, decay, att,
    s_send, p1_recv, p2_send, s_in, dec_send, dec_recv, power, mix, plain, scales, acc, starts,
    keys, values, queries, scores, probs, dens, o_send, o_recv,
    load_sem, p1_ss, p1_rs, dec_ss, dec_rs, p2_ss, p2_rs, pw_ss, pw_rs,
    kz_ss, kz_rs, qz_ss, qz_rs, vz_ss, vz_rs,
    ky_ss, ky_rs, kd_ss, kd_rs, vy_ss, vy_rs, vd_ss, vd_rs, sc_ss, sc_rs, o_ss, o_rs, out_sem,
):
    s = lax.axis_index("seq")
    t = lax.axis_index("tensor")
    z, y, x, c = s // NY, s % NY, t // 2, t % 2
    sib = 2 * x + (1 - c)

    barrier = pltpu.get_barrier_semaphore()
    partners = [((s + k) % SEQ, t) for k in range(1, SEQ)]
    partners += [(((z + k) % NZ) * NY + y, sib) for k in range(NZ)]
    partners += [(s, (2 * x + 2 * k + cc) % 8) for k in range(1, 4) for cc in range(2)]
    loads = []
    for n, (src, dst) in enumerate(
        ((decay_h, decay), (lk_h, lk), (lv_h, lv), (lq_h, lq), (gate_h, gate))
    ):
        cp = pltpu.make_async_copy(src, dst, load_sem.at[n])
        cp.start()
        loads.append(cp)
    for dev in partners:
        pl.semaphore_signal(barrier, inc=1, device_id=dev, device_id_type=MESH)

    pending = []

    def remote(src, dst, ss, rs, dev):
        cp = pltpu.make_async_remote_copy(
            src_ref=src, dst_ref=dst, send_sem=ss, recv_sem=rs, device_id=dev, device_id_type=MESH
        )
        return cp

    def send(src, dst, ss, rs, dev):
        cp = remote(src, dst, ss, rs, dev)
        cp.start()
        pending.append((cp, None))

    def send_or_keep(here, src, dst, ss, rs, dev):
        cp = remote(src, dst, ss, rs, dev)

        @pl.when(jnp.logical_not(here))
        def _():
            cp.start()

        @pl.when(here)
        def _():
            pltpu.make_async_copy(src, dst, rs).start()

        pending.append((cp, here))

    def arrived(dst, rs):
        pltpu.make_async_copy(dst, dst, rs).wait()

    ends = []
    total = jnp.int32(0)
    for d in range(DOCS):
        total = total + docs[d]
        ends.append(total)
    first = s * ROWS
    pos = first + iota((ROWS, 1), 0)
    start = doc_start(pos, ends)
    last_start = doc_start(first + ROWS - 1, ends)
    kept = (start < first).astype(F32)
    in_last = pos >= last_start

    loads[0].wait()
    lower = (iota((ROWS, ROWS), 1) <= iota((ROWS, ROWS), 0)).astype(BF16)
    rest = decay[...]
    running = jnp.zeros((ROWS, HEADS), F32)
    running_t = jnp.zeros((HEADS, ROWS), F32)
    for _ in range(3):
        part = rest.astype(BF16)
        rest = rest - part.astype(F32)
        running = running + mm(lower, part, ((1,), (1,)))
        running_t = running_t + mm(part, lower, ((1,), (1,)))
    final = running[ROWS - 1 : ROWS, :]
    fade = jnp.where(in_last, jnp.exp(jnp.minimum(final - running, 0.0)), 0.0)
    whole = jnp.where(last_start < first, jnp.exp(final), 0.0)
    for h in range(HEADS):
        dec_send[h] = jnp.broadcast_to(whole[:, h : h + 1], (1, HD))
    loads[1].wait()
    loads[2].wait()
    for h in range(HEADS):
        cols = slice(h * HD, (h + 1) * HD)
        faded = (lk[:, cols].astype(F32) * fade[:, h : h + 1]).astype(BF16)
        s_send[h * HD : (h + 1) * HD, :] = mm(faded, lv[:, cols], ((0,), (0,))).astype(BF16)

    pl.semaphore_wait(barrier, len(partners))

    piece = 16
    order = sorted(
        range(1, SEQ),
        key=lambda k: -min(k // NY, NZ - k // NY) - min(k % NY, NY - k % NY),
    )

    def ahead(k):
        return (z + k // NY) % NZ * NY + (y + k % NY) % NY

    def behind(k):
        return (z + NZ - k // NY) % NZ * NY + (y + NY - k % NY) % NY

    for k in order:
        p = ahead(k)
        send(dec_send.at[p // 8], dec_recv.at[s], dec_ss.at[k], dec_rs.at[k], (p, t))
        send(
            s_send.at[pl.ds(pl.multiple_of(p * piece, piece), piece)],
            p1_recv.at[s], p1_ss.at[k], p1_rs.at[k], (p, t),
        )
    dec_recv[s] = dec_send[s // 8]
    p1_recv[s] = s_send[pl.ds(pl.multiple_of(s * piece, piece), piece), :]

    def to_heads(src, dst, ss, rs):
        for n in range(HEADS):
            i = (z + n + 1) % HEADS
            for blk in range(2):
                zz = HEADS * c + i
                here = jnp.logical_and(zz == z, blk == c)
                send_or_keep(
                    here,
                    src.at[pl.ds(blk * HD, HD), pl.ds(pl.multiple_of(i * HD, HD), HD)],
                    dst(blk), ss.at[2 * n + blk], rs.at[z],
                    (zz * NY + y, 2 * x + blk),
                )

    to_heads(sk_h, lambda blk: keys.at[z, 2 * y + blk], kz_ss, kz_rs)

    loads[3].wait()
    lead = jnp.exp(running) * kept
    col = iota((1, ROWS), 1)
    allowed = (col <= iota((ROWS, 1), 0)) & (first + col >= start)
    for h in range(HEADS):
        cols = slice(h * HD, (h + 1) * HD)
        dots = mm(lq[:, cols], lk[:, cols], ((1,), (1,)))
        spread = jnp.where(allowed, running[:, h : h + 1] - running_t[h : h + 1, :], 0.0)
        weights = jnp.where(allowed, dots * jnp.exp(spread), 0.0).astype(BF16)
        att[:, cols] = mm(weights, lv[:, cols], ((1,), (0,)))

    for k in order:
        src = behind(k)
        arrived(dec_recv.at[src], dec_rs.at[k])
        arrived(p1_recv.at[src], p1_rs.at[k])
    state = jnp.zeros((piece, HD), F32)
    for r in range(SEQ):
        p2_send[r] = state.astype(BF16)
        state = dec_recv[r] * state + p1_recv[r].astype(F32)
    for k in order:
        p = ahead(k)
        send(p2_send.at[p], s_in.at[s], p2_ss.at[k], p2_rs.at[k], (p, t))
    s_in[s] = p2_send[s]
    to_heads(sq_h, lambda blk: queries.at[z], qz_ss, qz_rs)

    mine = 2 * y + c
    for k in NEAREST:
        zz = (z + k) % NZ
        arrived(keys.at[zz, mine], kz_rs.at[zz])
    for k in (1, 3):
        send(
            keys.at[:, mine], keys.at[:, mine], ky_ss.at[k], ky_rs.at[k],
            (z * NY + (y + k) % NY, t),
        )
    send(keys.at[:, mine], keys.at[:, mine], kd_ss.at[0], kd_rs.at[0], (s, sib))

    lane = iota((HD, HD), 1)
    for zt in range(NZ):
        row = zt * 1024 + y * ROWS + c * HD + iota((HD, 1), 0)
        starts[zt] = lane - doc_start(row, ends)
    dens[...] = jnp.full_like(dens, FLOOR)
    acc[...] = jnp.zeros_like(acc)
    for k in order:
        src = behind(k)
        arrived(s_in.at[src], p2_rs.at[k])
    loads[4].wait()
    power_col = jnp.zeros((ROWS, 1), F32)
    for h in range(HEADS):
        cols = slice(h * HD, (h + 1) * HD)
        state_h = s_in[h * 8 : (h + 1) * 8].reshape(HD, HD)
        carried = mm(lq[:, cols], state_h, ((1,), (0,)))
        full = att[:, cols] + lead[:, h : h + 1] * carried
        att[:, cols] = full
        power_col = power_col + jnp.sum(full * full, axis=1, keepdims=True)
    diag = iota((ROWS, ROWS), 0) == iota((ROWS, ROWS), 1)
    power[t] = jnp.sum(jnp.where(diag, power_col, 0.0), axis=0, keepdims=True)
    for k in range(1, 8):
        send(power.at[t], power.at[t], pw_ss.at[k], pw_rs.at[k], (s, (t + k) % 8))
    for h in range(HEADS):
        cols = slice(h * HD, (h + 1) * HD)
        gated = att[:, cols] * jax.nn.sigmoid(gate[:, cols].astype(F32))
        att[:, cols] = gated
        plain[:, cols] = gated.astype(BF16)
    to_heads(plain, lambda blk: values.at[z, 2 * y + blk], vz_ss, vz_rs)

    def spread_values(k):
        zz = (z + k) % NZ
        arrived(values.at[zz, mine], vz_rs.at[zz])
        for d in (2, 1, 3):
            send(
                values.at[zz, mine], values.at[zz, mine],
                vy_ss.at[k, d], vy_rs.at[zz, d], (z * NY + (y + d) % NY, t),
            )
        send(values.at[zz, mine], values.at[zz, mine], vd_ss.at[k, 0], vd_rs.at[zz, 0], (s, sib))

    def pass_values(k):
        zz = (z + k) % NZ
        for d in (1, 3, 2):
            block = 2 * ((y + NY - d) % NY) + c
            arrived(values.at[zz, block], vy_rs.at[zz, d])
            send(
                values.at[zz, block], values.at[zz, block],
                vd_ss.at[k, d], vd_rs.at[zz, d], (s, sib),
            )

    def finish_values(k):
        zz = (z + k) % NZ
        for d in range(NY):
            block = 2 * ((y + NY - d) % NY) + (1 - c)
            arrived(values.at[zz, block], vd_rs.at[zz, d])

    def weigh(k):
        zz = (z + k) % NZ

        def add(tiles):
            part = mm(
                probs[zz, 0:tiles].reshape(tiles * HD, 1024),
                values[zz].reshape(1024, HD), ((1,), (0,)),
            )
            at = pl.ds(zz, tiles)
            acc[at] = acc[at] + part.reshape(tiles, HD, HD)

        pl.when(zz < 4)(lambda: add(5))
        pl.when(zz >= 4)(lambda: add(4))


    def first_part(zt, d):
        side = (y + NY - d) % NY
        q = queries[zt]
        from_self = lane - (zt * 1024 + y * ROWS + c * HD) - iota((HD, HD), 0)
        from_start = starts[zt]
        top = dens[zt]
        for m in range(min(zt, 4) + 1):
            block = keys[zt - m, pl.ds(2 * side, 2)].reshape(256, HD)
            dots = mm(q, block, ((1,), (1,)))
            for half in range(2):
                place = side * 256 + half * HD
                base = (zt - m) * 1024 + place
                allowed = from_start >= -base
                if m == 0:
                    allowed = allowed & (from_self <= -base)
                part = jnp.where(allowed, dots[:, half * HD : (half + 1) * HD], FLOOR)
                scores[zt, m, :, pl.ds(pl.multiple_of(place, HD), HD)] = part
                top = jnp.maximum(top, part)
        dens[zt] = top

    def first_side(d):
        arrived(keys.at[:, 2 * ((y + NY - d) % NY) + (1 - c)], kd_rs.at[d])
        for zt in range(NZ):
            first_part(zt, d)

    def second_tile(zt):
        top = jnp.broadcast_to(jnp.max(dens[zt], axis=1, keepdims=True), (HD, HD))

        def group(m, den):
            for n in range(8):
                at = slice(n * HD, (n + 1) * HD)
                raised = jnp.exp2((scores[zt, m, :, at] - top) * EXPONENT)
                den = den + raised
                row = scales[(zt - m) * 4 + n // 2][:, (n % 2) * HD : (n % 2 + 1) * HD]
                probs[zt - m, m, :, at] = (raised * row).astype(BF16)
            return den

        den = lax.fori_loop(0, min(zt, 4) + 1, group, jnp.zeros((HD, HD), F32))
        dens[zt] = jnp.broadcast_to(jnp.sum(den, axis=1, keepdims=True), (HD, HD))

    spread_values(0)
    for k in (1, 3):
        block = 2 * ((y + NY - k) % NY) + c
        arrived(keys.at[:, block], ky_rs.at[k])
        half = slice(0, 4) if k == 1 else slice(4, 8)
        send(
            keys.at[half, block], keys.at[half, block], ky_ss.at[k - 1], ky_rs.at[k - 1],
            (z * NY + (y + k) % NY, t),
        )
        send(keys.at[:, block], keys.at[:, block], kd_ss.at[k], kd_rs.at[k], (s, sib))
    spread_values(1)
    spread_values(7)
    for k in range(1, 8):
        arrived(power.at[(t + 8 - k) % 8], pw_rs.at[k])
    total_row = power[0]
    for k in range(1, 8):
        total_row = total_row + power[k]
    scale_row = lax.rsqrt(total_row / (32 * HD) + 1e-06)
    scales[s] = scale_row
    for k in order:
        send(scales.at[s], scales.at[s], sc_ss.at[k], sc_rs.at[k], (ahead(k), t))
    spread_values(2)
    spread_values(6)
    scale = jnp.sum(jnp.where(diag, scale_row, 0.0), axis=1, keepdims=True)
    for h in range(HEADS):
        cols = slice(h * HD, (h + 1) * HD)
        mix[:, cols] = (att[:, cols] * scale).astype(BF16)
    mixed_copy = pltpu.make_async_copy(mix, mixed_h, out_sem.at[0])
    mixed_copy.start()
    spread_values(3)
    spread_values(5)
    spread_values(4)

    for zz in range(NZ):
        arrived(queries.at[zz], qz_rs.at[zz])
    first_side(0)
    across = 2 * ((y + 2) % NY) + c
    arrived(keys.at[0:4, across], ky_rs.at[0])
    arrived(keys.at[4:8, across], ky_rs.at[2])
    send(keys.at[:, across], keys.at[:, across], kd_ss.at[2], kd_rs.at[2], (s, sib))
    first_side(1)
    first_side(3)
    pass_values(0)
    first_side(2)
    pass_values(1)
    pass_values(7)
    for k in order:
        arrived(scales.at[behind(k)], sc_rs.at[k])
    for zt in range(4):
        second_tile(zt)
    pass_values(2)
    second_tile(4)
    pass_values(6)
    second_tile(5)
    pass_values(3)
    second_tile(6)
    pass_values(5)
    second_tile(7)
    for k in NEAREST[:5]:
        finish_values(k)
        weigh(k)
    pass_values(4)
    for k in NEAREST[5:]:
        finish_values(k)
        weigh(k)

    for k in reversed(NEAREST):
        zt = (z + k) % NZ
        o_send[zt] = (acc[zt] / dens[zt]).astype(BF16)
        src = o_send.at[zt]
        dst = o_recv.at[
            pl.ds(pl.multiple_of(c * HD, HD), HD),
            pl.ds(pl.multiple_of((z % HEADS) * HD, HD), HD),
        ]
        rs = o_rs.at[2 * (z % HEADS) + c]
        dev = (zt * NY + y, 2 * x + z // HEADS)
        if k:
            send(src, dst, o_ss.at[k], rs, dev)
        else:
            send_or_keep(z // HEADS == c, src, dst, o_ss.at[k], rs, dev)
    for i in range(HEADS):
        for blk in range(2):
            arrived(
                o_recv.at[pl.ds(blk * HD, HD), pl.ds(i * HD, HD)], o_rs.at[2 * i + blk]
            )
    out_copy = pltpu.make_async_copy(o_recv, out_h, out_sem.at[1])
    out_copy.start()
    for cp, here in pending:
        if here is None:
            cp.wait_send()
        else:
            pl.when(jnp.logical_not(here))(cp.wait_send)
    mixed_copy.wait()
    out_copy.wait()


def settle(a, b, c, d, a_held, b_held, sems):
    first = pltpu.make_async_copy(a, a_held, sems.at[0])
    second = pltpu.make_async_copy(b, b_held, sems.at[1])
    first.start()
    second.start()
    first.wait()
    first = pltpu.make_async_copy(a_held, c, sems.at[2])
    first.start()
    second.wait()
    second = pltpu.make_async_copy(b_held, d, sems.at[3])
    second.start()
    first.wait()
    second.wait()


def on_device(lq, lk, lv, gate, decay, sq, sk, docs):
    dma = pltpu.SemaphoreType.DMA
    vmem = pltpu.VMEM
    mixed, out = pl.pallas_call(
        kernel,
        out_shape=(
            jax.ShapeDtypeStruct((ROWS, WIDTH), BF16),
            jax.ShapeDtypeStruct((ROWS, WIDTH), BF16),
        ),
        in_specs=[pl.BlockSpec(memory_space=pltpu.SMEM)] + [pl.BlockSpec(memory_space=pltpu.HBM)] * 7,
        out_specs=(pl.BlockSpec(memory_space=pltpu.HBM), pl.BlockSpec(memory_space=pltpu.HBM)),
        scratch_shapes=[
            vmem((ROWS, WIDTH), BF16), vmem((ROWS, WIDTH), BF16),
            vmem((ROWS, WIDTH), BF16), vmem((ROWS, WIDTH), BF16),
            vmem((HEADS, ROWS), F32), vmem((ROWS, WIDTH), F32),
            vmem((WIDTH, HD), BF16), vmem((SEQ, 16, HD), BF16),
            vmem((SEQ, 16, HD), BF16), vmem((SEQ, 16, HD), BF16),
            vmem((HEADS, 1, HD), F32), vmem((SEQ, 1, HD), F32),
            vmem((8, 1, ROWS), F32), vmem((ROWS, WIDTH), BF16), vmem((ROWS, WIDTH), BF16),
            vmem((SEQ, 1, ROWS), F32), vmem((NZ + 3, HD, HD), F32),
            vmem((NZ, HD, HD), jnp.int32),
            vmem((NZ, 8, HD, HD), BF16), vmem((NZ, 8, HD, HD), BF16),
            vmem((NZ, HD, HD), BF16), vmem((NZ, 5, HD, 1024), F32),
            vmem((NZ, 5, HD, 1024), BF16), vmem((NZ, HD, HD), F32),
            vmem((NZ, HD, HD), BF16), vmem((ROWS, WIDTH), BF16),
            dma((5,)), dma((SEQ,)), dma((SEQ,)), dma((SEQ,)), dma((SEQ,)),
            dma((SEQ,)), dma((SEQ,)), dma((8,)), dma((8,)),
            dma((8,)), dma((8,)), dma((8,)), dma((8,)), dma((8,)), dma((8,)),
            dma((4,)), dma((4,)), dma((4,)), dma((4,)),
            dma((8, 4)), dma((8, 4)), dma((8, 4)), dma((8, 4)),
            dma((SEQ,)), dma((SEQ,)), dma((8,)), dma((8,)), dma((2,)),
        ],
        compiler_params=pltpu.CompilerParams(
            collective_id=0, has_side_effects=True, vmem_limit_bytes=(64 << 20) - (64 << 10)
        ),
    )(docs, lq, lk, lv, gate, decay.T, sq, sk)
    return pl.pallas_call(
        settle,
        out_shape=(
            jax.ShapeDtypeStruct((ROWS, WIDTH), BF16),
            jax.ShapeDtypeStruct((ROWS, WIDTH), BF16),
        ),
        in_specs=[pl.BlockSpec(memory_space=pl.ANY)] * 2,
        out_specs=(pl.BlockSpec(memory_space=pl.ANY), pl.BlockSpec(memory_space=pl.ANY)),
        scratch_shapes=[vmem((ROWS, WIDTH), BF16), vmem((ROWS, WIDTH), BF16), dma((4,))],
        compiler_params=pltpu.CompilerParams(vmem_limit_bytes=(64 << 20) - (64 << 10)),
    )(mixed, out)


def solution(mesh):
    split = P("seq", "tensor")
    return jax.shard_map(
        on_device,
        mesh=mesh,
        in_specs=(split,) * 7 + (P(),),
        out_specs=(split, split),
        check_vma=False,
    )
```

```python
import functools
import math

import jax
import jax.numpy as jnp
from jax import lax
from jax.experimental import pallas as pl
from jax.experimental.pallas import tpu as pltpu
from jax.sharding import PartitionSpec as P

MESH = pl.DeviceIdType.MESH
HD = 128
DOCS = 8
ROWS = 256
HEADS = 4
SEQ = 32
NZ = 8
NY = 4
WIDTH = HEADS * HD
FLOOR = -1e30
EXPONENT = math.log2(math.e) * HD**-0.5
NEAREST = (0, 1, 7, 2, 6, 3, 5, 4)
F32 = jnp.float32
BF16 = jnp.bfloat16


def mm(a, b, dims, precision=None):
    return lax.dot_general(
        a, b, (dims, ((), ())), preferred_element_type=F32, precision=precision
    )


def iota(shape, dim):
    return lax.broadcasted_iota(jnp.int32, shape, dim)


def doc_start(pos, ends):
    start = jnp.zeros_like(pos)
    for end in ends:
        start = jnp.where(pos >= end, end, start)
    return start


def kernel(
    docs, lq_h, lk_h, lv_h, gate_h, decay_h, sq_h, sk_h,
    mixed_h, out_h,
    lq, lk, lv, gate, decay, att,
    s_send, p1_recv, p2_send, s_in, dec_send, dec_recv, power, mix, plain, scales, acc, starts,
    keys, values, queries, scores, probs, dens, o_send, o_recv,
    load_sem, p1_ss, p1_rs, dec_ss, dec_rs, p2_ss, p2_rs, pw_ss, pw_rs,
    kz_ss, kz_rs, qz_ss, qz_rs, vz_ss, vz_rs,
    ky_ss, ky_rs, kd_ss, kd_rs, vy_ss, vy_rs, vd_ss, vd_rs, sc_ss, sc_rs, o_ss, o_rs, out_sem,
):
    s = lax.axis_index("seq")
    t = lax.axis_index("tensor")
    z, y, x, c = s // NY, s % NY, t // 2, t % 2
    sib = 2 * x + (1 - c)

    barrier = pltpu.get_barrier_semaphore()
    partners = [((s + k) % SEQ, t) for k in range(1, SEQ)]
    partners += [(((z + k) % NZ) * NY + y, sib) for k in range(NZ)]
    partners += [(s, (2 * x + 2 * k + cc) % 8) for k in range(1, 4) for cc in range(2)]
    loads = []
    for n, (src, dst) in enumerate(
        ((decay_h, decay), (lk_h, lk), (lv_h, lv), (lq_h, lq), (gate_h, gate))
    ):
        cp = pltpu.make_async_copy(src, dst, load_sem.at[n])
        cp.start()
        loads.append(cp)
    for dev in partners:
        pl.semaphore_signal(barrier, inc=1, device_id=dev, device_id_type=MESH)

    pending = []

    def remote(src, dst, ss, rs, dev):
        cp = pltpu.make_async_remote_copy(
            src_ref=src, dst_ref=dst, send_sem=ss, recv_sem=rs, device_id=dev, device_id_type=MESH
        )
        return cp

    def send(src, dst, ss, rs, dev):
        cp = remote(src, dst, ss, rs, dev)
        cp.start()
        pending.append((cp, None))

    def send_or_keep(here, src, dst, ss, rs, dev):
        cp = remote(src, dst, ss, rs, dev)

        @pl.when(jnp.logical_not(here))
        def _():
            cp.start()

        @pl.when(here)
        def _():
            pltpu.make_async_copy(src, dst, rs).start()

        pending.append((cp, here))

    def arrived(dst, rs):
        pltpu.make_async_copy(dst, dst, rs).wait()

    ends = []
    total = jnp.int32(0)
    for d in range(DOCS):
        total = total + docs[d]
        ends.append(total)
    first = s * ROWS
    pos = first + iota((ROWS, 1), 0)
    start = doc_start(pos, ends)
    last_start = doc_start(first + ROWS - 1, ends)
    kept = (start < first).astype(F32)
    in_last = pos >= last_start

    loads[0].wait()
    lower = (iota((ROWS, ROWS), 1) <= iota((ROWS, ROWS), 0)).astype(BF16)
    rest = decay[...]
    running = jnp.zeros((ROWS, HEADS), F32)
    running_t = jnp.zeros((HEADS, ROWS), F32)
    for _ in range(3):
        part = rest.astype(BF16)
        rest = rest - part.astype(F32)
        running = running + mm(lower, part, ((1,), (1,)))
        running_t = running_t + mm(part, lower, ((1,), (1,)))
    final = running[ROWS - 1 : ROWS, :]
    fade = jnp.where(in_last, jnp.exp(jnp.minimum(final - running, 0.0)), 0.0)
    whole = jnp.where(last_start < first, jnp.exp(final), 0.0)
    for h in range(HEADS):
        dec_send[h] = jnp.broadcast_to(whole[:, h : h + 1], (1, HD))
    loads[1].wait()
    loads[2].wait()
    for h in range(HEADS):
        cols = slice(h * HD, (h + 1) * HD)
        faded = (lk[:, cols].astype(F32) * fade[:, h : h + 1]).astype(BF16)
        s_send[h * HD : (h + 1) * HD, :] = mm(faded, lv[:, cols], ((0,), (0,))).astype(BF16)

    pl.semaphore_wait(barrier, len(partners))

    piece = 16
    order = sorted(
        range(1, SEQ),
        key=lambda k: -min(k // NY, NZ - k // NY) - min(k % NY, NY - k % NY),
    )

    def ahead(k):
        return (z + k // NY) % NZ * NY + (y + k % NY) % NY

    def behind(k):
        return (z + NZ - k // NY) % NZ * NY + (y + NY - k % NY) % NY

    for k in order:
        p = ahead(k)
        send(dec_send.at[p // 8], dec_recv.at[s], dec_ss.at[k], dec_rs.at[k], (p, t))
        send(
            s_send.at[pl.ds(pl.multiple_of(p * piece, piece), piece)],
            p1_recv.at[s], p1_ss.at[k], p1_rs.at[k], (p, t),
        )
    dec_recv[s] = dec_send[s // 8]
    p1_recv[s] = s_send[pl.ds(pl.multiple_of(s * piece, piece), piece), :]

    def to_heads(src, dst, ss, rs):
        for n in range(HEADS):
            i = (z + n + 1) % HEADS
            for blk in range(2):
                zz = HEADS * c + i
                here = jnp.logical_and(zz == z, blk == c)
                send_or_keep(
                    here,
                    src.at[pl.ds(blk * HD, HD), pl.ds(pl.multiple_of(i * HD, HD), HD)],
                    dst(blk), ss.at[2 * n + blk], rs.at[z],
                    (zz * NY + y, 2 * x + blk),
                )

    to_heads(sk_h, lambda blk: keys.at[z, 2 * y + blk], kz_ss, kz_rs)

    loads[3].wait()
    lead = jnp.exp(running) * kept
    col = iota((1, ROWS), 1)
    allowed = (col <= iota((ROWS, 1), 0)) & (first + col >= start)
    for h in range(HEADS):
        cols = slice(h * HD, (h + 1) * HD)
        dots = mm(lq[:, cols], lk[:, cols], ((1,), (1,)))
        spread = jnp.where(allowed, running[:, h : h + 1] - running_t[h : h + 1, :], 0.0)
        weights = jnp.where(allowed, dots * jnp.exp(spread), 0.0).astype(BF16)
        att[:, cols] = mm(weights, lv[:, cols], ((1,), (0,)))

    for k in order:
        src = behind(k)
        arrived(dec_recv.at[src], dec_rs.at[k])
        arrived(p1_recv.at[src], p1_rs.at[k])
    state = jnp.zeros((piece, HD), F32)
    for r in range(SEQ):
        p2_send[r] = state.astype(BF16)
        state = dec_recv[r] * state + p1_recv[r].astype(F32)
    for k in order:
        p = ahead(k)
        send(p2_send.at[p], s_in.at[s], p2_ss.at[k], p2_rs.at[k], (p, t))
    s_in[s] = p2_send[s]

    mine = 2 * y + c
    for k in NEAREST:
        zz = (z + k) % NZ
        arrived(keys.at[zz, mine], kz_rs.at[zz])
    for k in (1, 3):
        send(
            keys.at[:, mine], keys.at[:, mine], ky_ss.at[k], ky_rs.at[k],
            (z * NY + (y + k) % NY, t),
        )
    send(keys.at[:, mine], keys.at[:, mine], kd_ss.at[0], kd_rs.at[0], (s, sib))

    to_heads(sq_h, lambda blk: queries.at[z], qz_ss, qz_rs)
    lane = iota((HD, HD), 1)
    for zt in range(NZ):
        row = zt * 1024 + y * ROWS + c * HD + iota((HD, 1), 0)
        starts[zt] = lane - doc_start(row, ends)
    dens[...] = jnp.full_like(dens, FLOOR)
    acc[...] = jnp.zeros_like(acc)
    for k in order:
        src = behind(k)
        arrived(s_in.at[src], p2_rs.at[k])
    loads[4].wait()
    power_col = jnp.zeros((ROWS, 1), F32)
    for h in range(HEADS):
        cols = slice(h * HD, (h + 1) * HD)
        state_h = s_in[h * 8 : (h + 1) * 8].reshape(HD, HD)
        carried = mm(lq[:, cols], state_h, ((1,), (0,)))
        full = att[:, cols] + lead[:, h : h + 1] * carried
        att[:, cols] = full
        power_col = power_col + jnp.sum(full * full, axis=1, keepdims=True)
    diag = iota((ROWS, ROWS), 0) == iota((ROWS, ROWS), 1)
    power[t] = jnp.sum(jnp.where(diag, power_col, 0.0), axis=0, keepdims=True)
    for k in range(1, 8):
        send(power.at[t], power.at[t], pw_ss.at[k], pw_rs.at[k], (s, (t + k) % 8))
    for h in range(HEADS):
        cols = slice(h * HD, (h + 1) * HD)
        gated = att[:, cols] * jax.nn.sigmoid(gate[:, cols].astype(F32))
        att[:, cols] = gated
        plain[:, cols] = gated.astype(BF16)
    to_heads(plain, lambda blk: values.at[z, 2 * y + blk], vz_ss, vz_rs)

    def spread_values(k):
        zz = (z + k) % NZ
        arrived(values.at[zz, mine], vz_rs.at[zz])
        for d in (2, 1, 3):
            send(
                values.at[zz, mine], values.at[zz, mine],
                vy_ss.at[k, d], vy_rs.at[zz, d], (z * NY + (y + d) % NY, t),
            )
        send(values.at[zz, mine], values.at[zz, mine], vd_ss.at[k, 0], vd_rs.at[zz, 0], (s, sib))

    def pass_values(k):
        zz = (z + k) % NZ
        for d in (1, 3, 2):
            block = 2 * ((y + NY - d) % NY) + c
            arrived(values.at[zz, block], vy_rs.at[zz, d])
            send(
                values.at[zz, block], values.at[zz, block],
                vd_ss.at[k, d], vd_rs.at[zz, d], (s, sib),
            )

    def finish_values(k):
        zz = (z + k) % NZ
        for d in range(NY):
            block = 2 * ((y + NY - d) % NY) + (1 - c)
            arrived(values.at[zz, block], vd_rs.at[zz, d])

    def weigh(k):
        zz = (z + k) % NZ

        def add(tiles):
            part = mm(
                probs[zz, 0:tiles].reshape(tiles * HD, 1024),
                values[zz].reshape(1024, HD), ((1,), (0,)),
            )
            at = pl.ds(zz, tiles)
            acc[at] = acc[at] + part.reshape(tiles, HD, HD)

        pl.when(zz < 4)(lambda: add(5))
        pl.when(zz >= 4)(lambda: add(4))


    def first_part(zt, d):
        side = (y + NY - d) % NY
        q = queries[zt]
        from_self = lane - (zt * 1024 + y * ROWS + c * HD) - iota((HD, HD), 0)
        from_start = starts[zt]
        top = dens[zt]
        for m in range(min(zt, 4) + 1):
            block = keys[zt - m, pl.ds(2 * side, 2)].reshape(256, HD)
            dots = mm(q, block, ((1,), (1,)))
            for half in range(2):
                place = side * 256 + half * HD
                base = (zt - m) * 1024 + place
                allowed = from_start >= -base
                if m == 0:
                    allowed = allowed & (from_self <= -base)
                part = jnp.where(allowed, dots[:, half * HD : (half + 1) * HD], FLOOR)
                scores[zt, m, :, pl.ds(pl.multiple_of(place, HD), HD)] = part
                top = jnp.maximum(top, part)
        dens[zt] = top

    def first_side(d):
        arrived(keys.at[:, 2 * ((y + NY - d) % NY) + (1 - c)], kd_rs.at[d])
        for zt in range(NZ):
            first_part(zt, d)

    def second_tile(zt):
        top = jnp.broadcast_to(jnp.max(dens[zt], axis=1, keepdims=True), (HD, HD))

        def group(m, den):
            for n in range(8):
                at = slice(n * HD, (n + 1) * HD)
                raised = jnp.exp2((scores[zt, m, :, at] - top) * EXPONENT)
                den = den + raised
                row = scales[(zt - m) * 4 + n // 2][:, (n % 2) * HD : (n % 2 + 1) * HD]
                probs[zt - m, m, :, at] = (raised * row).astype(BF16)
            return den

        den = lax.fori_loop(0, min(zt, 4) + 1, group, jnp.zeros((HD, HD), F32))
        dens[zt] = jnp.broadcast_to(jnp.sum(den, axis=1, keepdims=True), (HD, HD))

    spread_values(0)
    for k in (1, 3):
        block = 2 * ((y + NY - k) % NY) + c
        arrived(keys.at[:, block], ky_rs.at[k])
        half = slice(0, 4) if k == 1 else slice(4, 8)
        send(
            keys.at[half, block], keys.at[half, block], ky_ss.at[k - 1], ky_rs.at[k - 1],
            (z * NY + (y + k) % NY, t),
        )
        send(keys.at[:, block], keys.at[:, block], kd_ss.at[k], kd_rs.at[k], (s, sib))
    spread_values(1)
    spread_values(7)
    for k in range(1, 8):
        arrived(power.at[(t + 8 - k) % 8], pw_rs.at[k])
    total_row = power[0]
    for k in range(1, 8):
        total_row = total_row + power[k]
    scale_row = lax.rsqrt(total_row / (32 * HD) + 1e-06)
    scales[s] = scale_row
    for k in order:
        send(scales.at[s], scales.at[s], sc_ss.at[k], sc_rs.at[k], (ahead(k), t))
    spread_values(2)
    spread_values(6)
    scale = jnp.sum(jnp.where(diag, scale_row, 0.0), axis=1, keepdims=True)
    for h in range(HEADS):
        cols = slice(h * HD, (h + 1) * HD)
        mix[:, cols] = (att[:, cols] * scale).astype(BF16)
    mixed_copy = pltpu.make_async_copy(mix, mixed_h, out_sem.at[0])
    mixed_copy.start()
    spread_values(3)
    spread_values(5)
    spread_values(4)

    for zz in range(NZ):
        arrived(queries.at[zz], qz_rs.at[zz])
    first_side(0)
    across = 2 * ((y + 2) % NY) + c
    arrived(keys.at[0:4, across], ky_rs.at[0])
    arrived(keys.at[4:8, across], ky_rs.at[2])
    send(keys.at[:, across], keys.at[:, across], kd_ss.at[2], kd_rs.at[2], (s, sib))
    first_side(1)
    first_side(3)
    pass_values(0)
    first_side(2)
    pass_values(1)
    pass_values(7)
    for k in order:
        arrived(scales.at[behind(k)], sc_rs.at[k])
    for zt in range(4):
        second_tile(zt)
    pass_values(2)
    second_tile(4)
    pass_values(6)
    second_tile(5)
    pass_values(3)
    second_tile(6)
    pass_values(5)
    second_tile(7)
    for k in NEAREST[:5]:
        finish_values(k)
        weigh(k)
    pass_values(4)
    for k in NEAREST[5:]:
        finish_values(k)
        weigh(k)

    for k in reversed(NEAREST):
        zt = (z + k) % NZ
        o_send[zt] = (acc[zt] / dens[zt]).astype(BF16)
        src = o_send.at[zt]
        dst = o_recv.at[
            pl.ds(pl.multiple_of(c * HD, HD), HD),
            pl.ds(pl.multiple_of((z % HEADS) * HD, HD), HD),
        ]
        rs = o_rs.at[2 * (z % HEADS) + c]
        dev = (zt * NY + y, 2 * x + z // HEADS)
        if k:
            send(src, dst, o_ss.at[k], rs, dev)
        else:
            send_or_keep(z // HEADS == c, src, dst, o_ss.at[k], rs, dev)
    for i in range(HEADS):
        for blk in range(2):
            arrived(
                o_recv.at[pl.ds(blk * HD, HD), pl.ds(i * HD, HD)], o_rs.at[2 * i + blk]
            )
    out_copy = pltpu.make_async_copy(o_recv, out_h, out_sem.at[1])
    out_copy.start()
    for cp, here in pending:
        if here is None:
            cp.wait_send()
        else:
            pl.when(jnp.logical_not(here))(cp.wait_send)
    mixed_copy.wait()
    out_copy.wait()


def settle(a, b, c, d, a_held, b_held, sems):
    first = pltpu.make_async_copy(a, a_held, sems.at[0])
    second = pltpu.make_async_copy(b, b_held, sems.at[1])
    first.start()
    second.start()
    first.wait()
    first = pltpu.make_async_copy(a_held, c, sems.at[2])
    first.start()
    second.wait()
    second = pltpu.make_async_copy(b_held, d, sems.at[3])
    second.start()
    first.wait()
    second.wait()


def on_device(lq, lk, lv, gate, decay, sq, sk, docs):
    dma = pltpu.SemaphoreType.DMA
    vmem = pltpu.VMEM
    mixed, out = pl.pallas_call(
        kernel,
        out_shape=(
            jax.ShapeDtypeStruct((ROWS, WIDTH), BF16),
            jax.ShapeDtypeStruct((ROWS, WIDTH), BF16),
        ),
        in_specs=[pl.BlockSpec(memory_space=pltpu.SMEM)] + [pl.BlockSpec(memory_space=pltpu.HBM)] * 7,
        out_specs=(pl.BlockSpec(memory_space=pltpu.HBM), pl.BlockSpec(memory_space=pltpu.HBM)),
        scratch_shapes=[
            vmem((ROWS, WIDTH), BF16), vmem((ROWS, WIDTH), BF16),
            vmem((ROWS, WIDTH), BF16), vmem((ROWS, WIDTH), BF16),
            vmem((HEADS, ROWS), F32), vmem((ROWS, WIDTH), F32),
            vmem((WIDTH, HD), BF16), vmem((SEQ, 16, HD), BF16),
            vmem((SEQ, 16, HD), BF16), vmem((SEQ, 16, HD), BF16),
            vmem((HEADS, 1, HD), F32), vmem((SEQ, 1, HD), F32),
            vmem((8, 1, ROWS), F32), vmem((ROWS, WIDTH), BF16), vmem((ROWS, WIDTH), BF16),
            vmem((SEQ, 1, ROWS), F32), vmem((NZ + 3, HD, HD), F32),
            vmem((NZ, HD, HD), jnp.int32),
            vmem((NZ, 8, HD, HD), BF16), vmem((NZ, 8, HD, HD), BF16),
            vmem((NZ, HD, HD), BF16), vmem((NZ, 5, HD, 1024), F32),
            vmem((NZ, 5, HD, 1024), BF16), vmem((NZ, HD, HD), F32),
            vmem((NZ, HD, HD), BF16), vmem((ROWS, WIDTH), BF16),
            dma((5,)), dma((SEQ,)), dma((SEQ,)), dma((SEQ,)), dma((SEQ,)),
            dma((SEQ,)), dma((SEQ,)), dma((8,)), dma((8,)),
            dma((8,)), dma((8,)), dma((8,)), dma((8,)), dma((8,)), dma((8,)),
            dma((4,)), dma((4,)), dma((4,)), dma((4,)),
            dma((8, 4)), dma((8, 4)), dma((8, 4)), dma((8, 4)),
            dma((SEQ,)), dma((SEQ,)), dma((8,)), dma((8,)), dma((2,)),
        ],
        compiler_params=pltpu.CompilerParams(
            collective_id=0, has_side_effects=True, vmem_limit_bytes=(64 << 20) - (64 << 10)
        ),
    )(docs, lq, lk, lv, gate, decay.T, sq, sk)
    return pl.pallas_call(
        settle,
        out_shape=(
            jax.ShapeDtypeStruct((ROWS, WIDTH), BF16),
            jax.ShapeDtypeStruct((ROWS, WIDTH), BF16),
        ),
        in_specs=[pl.BlockSpec(memory_space=pl.ANY)] * 2,
        out_specs=(pl.BlockSpec(memory_space=pl.ANY), pl.BlockSpec(memory_space=pl.ANY)),
        scratch_shapes=[vmem((ROWS, WIDTH), BF16), vmem((ROWS, WIDTH), BF16), dma((4,))],
        compiler_params=pltpu.CompilerParams(vmem_limit_bytes=(64 << 20) - (64 << 10)),
    )(mixed, out)


def solution(mesh):
    split = P("seq", "tensor")
    return jax.shard_map(
        on_device,
        mesh=mesh,
        in_specs=(split,) * 7 + (P(),),
        out_specs=(split, split),
        check_vma=False,
    )
```
